128 devices in a mesh: dp: 16 (over y, x), expert: 8 (over z, core).
Axes of the slice: x: 4, y: 4, z: 4, core: 2. Of those that a mesh axis runs over, the one named last changes fastest.
Arguments:
- layer_input: bfloat16 [4096, 2048], P(('dp', 'expert')), may hold values from -6 to 6
- out_grad: bfloat16 [4096, 2048], P(('dp', 'expert')), may hold values from -3 to 3
- routes: int32 [4096, 8], P(('dp', 'expert')), may hold values from 0 to 15, all different within a row
- probs: bfloat16 [4096, 8], P(('dp', 'expert')), may hold values from 0.049804688 to 1
- gate_up: bfloat16 [2048, 2, 16, 768], P(None, None, 'expert'), may hold values from -0.125 to 0.125
- down_t: bfloat16 [2048, 16, 768], P(None, 'expert'), may hold values from -0.21875 to 0.21875
Outputs:
- grad_input: bfloat16 [4096, 2048], P(('dp', 'expert'))
- grad_prob: float32 [4096, 8], P(('dp', 'expert'))
- grad_weights: bfloat16 [2048, 3, 16, 768], P('dp', None, 'expert')
The draws below stay inside these ranges and needn't reach their ends.
Inputs may be any that keep to these rules, and one draw needn't show every extreme that they name: `routes`: each row names 8 different experts.
All inputs are finite; a program needn't handle non-finite values. Where the reference program divides by a largest or mean magnitude, that divisor is 1e-20 or more.
Results may differ from the reference program's by a relative error of at most 0.02.
Values may be sent and summed in bfloat16 or wider, within the bound.
No kernel may reach another device: no remote copies, remote signals or barrier semaphores. Data moves between devices by JAX's collectives and lax.ppermute only.
A program may use at most 256 MiB of HBM per device.

```python
import math
import jax
import jax.numpy as jnp
from jax import lax

D = 2048
FF = 768
EXPERTS = 16
TOP = 8
BLOCK = 128
TOK_DEV = 32
TOKENS = 4096
N_DP = 16
N_EXPERT = 8


def shard_levels(rng, dims, cuts, smallest, top_value):
    loudness, own = 1.0, jax.random.fold_in(rng, 6)
    for dim, blocks in cuts:
        steps = jnp.exp(jax.random.uniform(jax.random.fold_in(own, dim), (blocks,), jnp.float32, smallest / len(cuts), top_value / len(cuts)))
        loudness = loudness * jnp.repeat(steps, dims[dim] // blocks).reshape([-1 if axis == dim else 1 for axis in range(len(dims))])
    return loudness


def picks_of(rng, rows, count, top, lift):
    order = jax.random.permutation(jax.random.fold_in(rng, 1), count)
    favour = order
    for power in range(3):
        favour = favour * favour // count
    favour = favour * lift // count
    tickets = jax.random.randint(jax.random.fold_in(rng, 2), (rows, count), 0, 4096) + favour
    holders = jax.random.permutation(jax.random.fold_in(rng, 3), rows)[jnp.arange(count) % rows]
    tickets = jnp.where(jnp.arange(rows)[:, None] == holders[None, :], 1 << 14, tickets)
    score = tickets * count + jnp.arange(count)
    return lax.top_k(score.astype(jnp.int32), top)[1].astype(jnp.int32)


def bell_draw(stream_key, dims, deviation, reach, pieces=(), kind=jnp.bfloat16):
    drawn = deviation * jax.random.normal(stream_key, dims, jnp.float32)
    if pieces:
        drawn = drawn * shard_levels(stream_key, dims, pieces, -0.22, 0.18)
    return jnp.clip(drawn, -reach, reach).astype(kind)


def setup_inputs(seed: int = 0) -> dict:
    arg_keys = jax.random.split(jax.random.key(seed), 7)
    layer_input = bell_draw(arg_keys[0], (TOKENS, D), 1.0, 6.0, ((0, 128),))
    out_grad = bell_draw(arg_keys[1], (TOKENS, D), 0.5, 3.0, ((0, 128),))
    routes = picks_of(arg_keys[2], TOKENS, EXPERTS, TOP, 8192)
    probs = jnp.clip(jnp.exp(math.log(1.0) - 2.9996462 * jax.random.uniform(arg_keys[3], (TOKENS, TOP), jnp.float32) ** shard_levels(arg_keys[3], (TOKENS, TOP), ((0, 128),), -0.2, 0.2)), 0.049804688, 1.0).astype(jnp.bfloat16)
    gate_up = bell_draw(arg_keys[4], (D, 2, EXPERTS, FF), D ** -0.5, 0.125, ((2, 8),))
    down_t = bell_draw(arg_keys[5], (D, EXPERTS, FF), FF ** -0.5, 0.21875, ((1, 8),))
    return {"layer_input": layer_input, "out_grad": out_grad, "routes": routes, "probs": probs, "gate_up": gate_up, "down_t": down_t}


def slots_of(block_routes):
    flat_routes = block_routes.reshape(-1)
    onehot = (flat_routes[:, None] == jnp.arange(EXPERTS, dtype=jnp.int32)[None, :]).astype(jnp.int32)
    before = jnp.cumsum(onehot, axis=0) - onehot
    ranks = jnp.sum(before * onehot, axis=1)
    return (flat_routes * TOK_DEV + ranks).astype(jnp.int32)


def place_rows(values, slots):
    empty = jnp.zeros((EXPERTS * TOK_DEV,) + values.shape[1:], values.dtype)
    return empty.at[slots].set(values)


def to_experts(per_source):
    shaped = per_source.reshape((N_EXPERT, EXPERTS, TOK_DEV) + per_source.shape[2:])
    moved = jnp.moveaxis(shaped, 0, 1)
    return moved.reshape((EXPERTS, N_EXPERT * TOK_DEV) + per_source.shape[2:])


def to_sources(per_expert):
    shaped = per_expert.reshape((EXPERTS, N_EXPERT, TOK_DEV) + per_expert.shape[2:])
    moved = jnp.moveaxis(shaped, 1, 0)
    return moved.reshape((N_EXPERT, EXPERTS * TOK_DEV) + per_expert.shape[3:])


def expert_math(rows_x, rows_dy, rows_p, weight_gate, weight_up, weight_down):
    input_f = rows_x.astype(jnp.float32)
    grad_f = rows_dy.astype(jnp.float32)
    gate_pre = jnp.einsum('esd,def->esf', input_f, weight_gate)
    up_pre = jnp.einsum('esd,def->esf', input_f, weight_up)
    sigmoid_gate = jax.nn.sigmoid(gate_pre)
    activated = gate_pre * sigmoid_gate
    hidden = (activated * up_pre).astype(jnp.bfloat16)
    hidden_f = hidden.astype(jnp.float32)
    expert_out = jnp.einsum('esf,def->esd', hidden_f, weight_down)
    prob_grad = jnp.sum(grad_f * expert_out, axis=-1)
    back_proj = jnp.einsum('esd,def->esf', grad_f, weight_down)
    weight_p = rows_p.astype(jnp.float32)[..., None]
    hidden_grad = weight_p * back_proj
    scaled = (weight_p * grad_f).astype(jnp.bfloat16)
    gate_grad = (hidden_grad * up_pre * sigmoid_gate * (1.0 + gate_pre * (1.0 - sigmoid_gate))).astype(jnp.bfloat16)
    up_grad = (hidden_grad * activated).astype(jnp.bfloat16)
    slot_grad = jnp.einsum('esf,def->esd', gate_grad.astype(jnp.float32), weight_gate)
    slot_grad = slot_grad + jnp.einsum('esf,def->esd', up_grad.astype(jnp.float32), weight_up)
    blocks = slot_grad.reshape(slot_grad.shape[0], slot_grad.shape[1], D // BLOCK, BLOCK)
    block_scale = jnp.max(jnp.abs(blocks), axis=-1) + 1e-6
    packed = (blocks / block_scale[..., None]).astype(jnp.bfloat16).reshape(slot_grad.shape)
    term_gate = jnp.einsum('esd,esf->def', input_f, gate_grad.astype(jnp.float32))
    term_up = jnp.einsum('esd,esf->def', input_f, up_grad.astype(jnp.float32))
    term_down = jnp.einsum('esd,esf->def', scaled.astype(jnp.float32), hidden_f)
    terms = jnp.stack([term_gate, term_up, term_down], axis=1)
    return packed, block_scale, prob_grad, terms


def reference(layer_input, out_grad, routes, probs, gate_up, down_t):
    weight_gate = gate_up[:, 0].astype(jnp.float32)
    weight_up = gate_up[:, 1].astype(jnp.float32)
    weight_down = down_t.astype(jnp.float32)
    input_blocks = layer_input.reshape(N_DP, N_EXPERT, TOK_DEV, D)
    grad_blocks = out_grad.reshape(N_DP, N_EXPERT, TOK_DEV, D)
    route_blocks = routes.reshape(N_DP, N_EXPERT, TOK_DEV, TOP)
    prob_blocks = probs.reshape(N_DP, N_EXPERT, TOK_DEV * TOP)

    def one_group(carry, blocks):
        group_x, group_dy, group_routes, group_p = blocks
        slots = jax.vmap(slots_of)(group_routes)
        send_x = jax.vmap(place_rows)(jnp.repeat(group_x, TOP, axis=1), slots)
        send_dy = jax.vmap(place_rows)(jnp.repeat(group_dy, TOP, axis=1), slots)
        send_p = jax.vmap(place_rows)(group_p, slots)
        packed, block_scale, prob_grad, terms = expert_math(
            to_experts(send_x), to_experts(send_dy), to_experts(send_p),
            weight_gate, weight_up, weight_down)
        rounded = lax.optimization_barrier(terms.astype(jnp.bfloat16)).astype(jnp.float32)
        back_rows = to_sources(packed[:, :, None, :])
        back_scale = to_sources(block_scale[:, :, None, :])
        back_prob = to_sources(prob_grad[:, :, None])

        def combine(rows, scales, prob_rows, slot):
            picked = rows[slot].astype(jnp.float32).reshape(TOK_DEV * TOP, D // BLOCK, BLOCK)
            restored = (picked * scales[slot][:, :, None]).reshape(TOK_DEV, TOP, D)
            return jnp.sum(restored, axis=1).astype(jnp.bfloat16), prob_rows[slot].reshape(TOK_DEV, TOP)

        grads, prob_out = jax.vmap(combine)(back_rows, back_scale, back_prob, slots)
        return carry + rounded, (grads, prob_out)

    start = jnp.zeros((D, 3, EXPERTS, FF), jnp.float32)
    total, outs = lax.scan(one_group, start, (input_blocks, grad_blocks, route_blocks, prob_blocks))
    grad_input = outs[0].reshape(TOKENS, D)
    grad_prob = outs[1].reshape(TOKENS, TOP)
    return grad_input, grad_prob, total.astype(jnp.bfloat16)
```

```python
import functools

import jax
import jax.numpy as jnp
import numpy as np
from jax import lax
from jax.experimental import pallas as pl
from jax.experimental.pallas import tpu as pltpu
from jax.sharding import Mesh, PartitionSpec as P

F32 = jnp.float32
BF16 = jnp.bfloat16
LANES = 128
SIDE = 4
VMEM = 48 << 20

XOR = {k: [(j, j ^ k) for j in range(SIDE)] for k in (1, 2, 3)}
RIGHT = [(j, (j + 1) % SIDE) for j in range(SIDE)]
LEFT = [(j, (j - 1) % SIDE) for j in range(SIDE)]
SWAP = [(0, 1), (1, 0)]


def forward_kernel(width, mine_ref, other_ref, sel_ref, gate_ref, up_ref, down_ref, h_ref, gp_ref, rows_ref):
    step = pl.program_id(0)
    half = mine_ref.shape[0]

    @pl.when(step == 0)
    def _():
        rows_ref[:half] = mine_ref[...]
        rows_ref[half:] = other_ref[...]

    block = 256
    for start in range(0, 2 * half, block):
        rows = pl.ds(start, block)
        x = rows_ref[rows, :width]
        dy = rows_ref[rows, width : 2 * width]
        p = jnp.sum(rows_ref[rows, 2 * width :].astype(F32) * sel_ref[...], axis=-1, keepdims=True)
        gate = jnp.dot(x, gate_ref[...], preferred_element_type=F32)
        up = jnp.dot(x, up_ref[...], preferred_element_type=F32)
        back = jnp.dot(dy, down_ref[...], preferred_element_type=F32)
        sig = 1.0 / (1.0 + jnp.exp(-gate))
        act = gate * sig
        hidden = act * up
        hidden_grad = p * back
        h_ref[0, rows] = (hidden_grad * up * (sig * (1.0 + gate * (1.0 - sig)))).astype(BF16)
        h_ref[1, rows] = (hidden_grad * act).astype(BF16)
        h_ref[2, rows] = (p * hidden).astype(BF16)
        term = jnp.sum(hidden * back, axis=-1, keepdims=True) * sel_ref[...]

        @pl.when(step == 0)
        def _():
            gp_ref[rows] = term

        @pl.when(step != 0)
        def _():
            gp_ref[rows] = gp_ref[rows] + term


def forward(mine, other, sel, gate_up, down):
    half, columns = mine.shape
    width, hidden = down.shape
    rows = 2 * half
    tile = 256
    return pl.pallas_call(
        functools.partial(forward_kernel, width),
        name="forward",
        grid=(hidden // tile,),
        in_specs=[
            pl.BlockSpec((half, columns), lambda j: (0, 0)),
            pl.BlockSpec((half, columns), lambda j: (0, 0)),
            pl.BlockSpec((1, LANES), lambda j: (0, 0)),
            pl.BlockSpec((None, width, tile), lambda j: (0, 0, j)),
            pl.BlockSpec((None, width, tile), lambda j: (1, 0, j)),
            pl.BlockSpec((width, tile), lambda j: (0, j)),
        ],
        out_specs=[
            pl.BlockSpec((3, rows, tile), lambda j: (0, 0, j)),
            pl.BlockSpec((rows, LANES), lambda j: (0, 0)),
        ],
        out_shape=[
            jax.ShapeDtypeStruct((3, rows, hidden), BF16),
            jax.ShapeDtypeStruct((rows, LANES), F32),
        ],
        scratch_shapes=[pltpu.VMEM((rows, columns), BF16)],
        compiler_params=pltpu.CompilerParams(vmem_limit_bytes=VMEM),
        cost_estimate=pl.CostEstimate(
            flops=6 * rows * width * hidden, bytes_accessed=6 * width * hidden, transcendentals=0
        ),
    )(mine, other, sel, gate_up, gate_up, down)


def weight_kernel(pieces, spans, cols_ref, *refs):
    col_refs = refs[: 4 * pieces]
    h_refs = refs[4 * pieces : 4 * pieces + pieces // 2]
    out_ref, x_ref, dy_ref = refs[4 * pieces + pieces // 2 :]
    at = 0
    for piece, span in enumerate(spans):
        x_other, x_own, dy_other, dy_own = col_refs[4 * piece : 4 * piece + 4]
        rows = pl.ds(at, span)
        x_ref[rows, :LANES] = x_other[...]
        x_ref[rows, LANES:] = x_own[...]
        dy_ref[rows, :LANES] = dy_other[...]
        dy_ref[rows, LANES:] = dy_own[...]
        at += span
    contract = (((0,), (0,)), ((), ()))
    for kind, source in enumerate((x_ref, x_ref, dy_ref)):
        total = None
        at = 0
        for chunk in range(pieces // 2):
            span = 2 * spans[2 * chunk]
            term = lax.dot_general(
                source[at : at + span], h_refs[chunk][kind], contract, preferred_element_type=F32
            )
            total = term if total is None else total + term
            at += span
        out_ref[0, kind] = total[:LANES].astype(BF16)
        out_ref[1, kind] = total[LANES:].astype(BF16)


def weight_terms(cols, chunks, hs):
    steps = cols.shape[0] // 4
    hidden = hs[0].shape[2]
    arrays, specs, spans = [], [], []
    for pair in chunks:
        for rows in pair:
            spans.append(rows.shape[0])
            for which in range(4):
                arrays.append(rows)
                specs.append(
                    pl.BlockSpec(
                        (rows.shape[0], LANES), lambda j, cols, which=which: (0, cols[4 * j + which])
                    )
                )
    for h in hs:
        arrays.append(h)
        specs.append(pl.BlockSpec(h.shape, lambda j, cols: (0, 0, 0)))
    tokens = sum(spans)
    return pl.pallas_call(
        functools.partial(weight_kernel, len(spans), tuple(spans)),
        name="weight_terms",
        grid_spec=pltpu.PrefetchScalarGridSpec(
            num_scalar_prefetch=1,
            grid=(steps,),
            in_specs=specs,
            out_specs=pl.BlockSpec((None, 2, 3, LANES, hidden), lambda j, cols: (j, 0, 0, 0, 0)),
            scratch_shapes=[pltpu.VMEM((tokens, 2 * LANES), BF16), pltpu.VMEM((tokens, 2 * LANES), BF16)],
        ),
        out_shape=jax.ShapeDtypeStruct((steps, 2, 3, LANES, hidden), BF16),
        compiler_params=pltpu.CompilerParams(vmem_limit_bytes=VMEM),
        cost_estimate=pl.CostEstimate(
            flops=12 * steps * tokens * LANES * hidden,
            bytes_accessed=6 * tokens * hidden,
            transcendentals=0,
        ),
    )(cols, *arrays)


def slot_rows(sub, side):
    order = []
    for z in range(SIDE):
        for x in range(2):
            if z == 0:
                order.append((0, x * sub))
            elif z < 3:
                order.append((1, (z - 1) * SIDE * sub + x * sub))
            else:
                order.append((2, x * sub))
            order.append((0, SIDE * sub + z * sub) if x == 0 else (1, 2 * SIDE * sub + z * sub))
    return order


def slot_kernel(sub, width, h1, h2, h3, g1, g2, g3, gate_ref, up_ref, mine_ref, other_ref, rows_ref):
    step = pl.program_id(0)
    hs, gs = (h1, h2, h3), (g1, g2, g3)
    half = rows_ref.shape[1] // 2

    @pl.when(step == 0)
    def _():
        for core, out in enumerate((mine_ref, other_ref)):
            for n, (chunk, first) in enumerate(slot_rows(sub, SIDE)):
                at = first + core * (hs[chunk].shape[1] // 2)
                for kind in range(2):
                    rows_ref[kind, core * half + n * sub : core * half + (n + 1) * sub] = hs[chunk][
                        kind, at : at + sub
                    ]
                out[n * sub : (n + 1) * sub, width:] = gs[chunk][at : at + sub].astype(BF16)

    contract = (((1,), (1,)), ((), ()))
    tile = gate_ref.shape[0]
    cols = pl.ds(pl.multiple_of(step * tile, tile), tile)
    for core, out in enumerate((mine_ref, other_ref)):
        rows = slice(core * half, (core + 1) * half)
        total = lax.dot_general(rows_ref[0, rows], gate_ref[...], contract, preferred_element_type=F32)
        total += lax.dot_general(rows_ref[1, rows], up_ref[...], contract, preferred_element_type=F32)
        out[:, cols] = total.astype(BF16)


def slot_terms(hs, gps, gate_up, sub):
    _, width, hidden = gate_up.shape
    tile = 512
    half = 16 * sub
    out = jax.ShapeDtypeStruct((half, width + LANES), BF16)
    specs = [pl.BlockSpec((2,) + h.shape[1:], lambda j: (0, 0, 0)) for h in hs]
    specs += [pl.BlockSpec(g.shape, lambda j: (0, 0)) for g in gps]
    specs += [pl.BlockSpec((None, tile, hidden), lambda j, k=k: (k, j, 0)) for k in range(2)]
    return pl.pallas_call(
        functools.partial(slot_kernel, sub, width),
        name="slot_terms",
        grid=(width // tile,),
        in_specs=specs,
        out_specs=[pl.BlockSpec(out.shape, lambda j: (0, 0))] * 2,
        out_shape=[out, out],
        scratch_shapes=[pltpu.VMEM((2, 2 * half, hidden), BF16)],
        compiler_params=pltpu.CompilerParams(vmem_limit_bytes=VMEM),
        cost_estimate=pl.CostEstimate(
            flops=8 * half * width * hidden, bytes_accessed=4 * width * hidden, transcendentals=0
        ),
    )(*hs, *gps, gate_up, gate_up)


def add(a, b):
    return (a.astype(F32) + b.astype(F32)).astype(BF16)


def shards(layer_input, out_grad, routes, probs, gate_up, down_t):
    tokens, width = layer_input.shape
    sub = tokens // 2
    x, y = lax.axis_index("x"), lax.axis_index("y")
    z, core = lax.axis_index("z"), lax.axis_index("core")
    expert = x % 2
    lane = lax.broadcasted_iota(jnp.int32, (1, LANES), 1)
    sel = (lane == (z * 2 + core) * 2 + expert).astype(F32)

    hot = routes[:, :, None] == lax.broadcasted_iota(jnp.int32, (1, 1, LANES), 2)
    dense = jnp.sum(jnp.where(hot, probs.astype(F32)[:, :, None], 0.0), axis=1).astype(BF16)
    row = jnp.concatenate([layer_input, out_grad, dense], axis=1)

    first, second = row[:sub], row[sub:]
    near = [1, 3, 2]
    first_x = [first] + [lax.ppermute(first, "x", XOR[k]) for k in near]
    second_z = [second] + [lax.ppermute(second, "z", XOR[k]) for k in near]
    first_x = jnp.concatenate(first_x, axis=0)
    second_z = jnp.concatenate(second_z, axis=0)
    first_z = [lax.ppermute(first_x, "z", XOR[k]) for k in near]
    second_x = [lax.ppermute(second_z, "x", XOR[k]) for k in near]

    mine = [
        jnp.concatenate([first_x, second_z], axis=0),
        jnp.concatenate(first_z[:2] + second_x[:2], axis=0),
        jnp.concatenate([first_z[2], second_x[2]], axis=0),
    ]
    chunks = [(m, lax.ppermute(m, "core", SWAP)) for m in mine]

    gate_up = jnp.transpose(lax.dynamic_index_in_dim(gate_up, expert, 2, keepdims=False), (1, 0, 2))
    down = lax.dynamic_index_in_dim(down_t, expert, 1, keepdims=False)

    hs, gps = [], []
    for m, o in chunks:
        h, gp = forward(m, o, sel, gate_up, down)
        hs.append(h)
        gps.append(gp)

    blocks = width // LANES
    cols = []
    for r in (2, 3, 1, 0):
        base = SIDE * ((y + r) % SIDE)
        other, own = base + (x ^ 1), base + x
        cols += [other, own, blocks + other, blocks + own]
    cols = jnp.stack(cols).astype(jnp.int32)
    far = weight_terms(cols[:8], chunks, hs)
    close = weight_terms(cols[8:], chunks, hs)

    a_right = lax.ppermute(far[0, 0], "y", RIGHT)
    a_left = lax.ppermute(far[1, 0], "y", LEFT)
    b_left = lax.ppermute(far[0, 1], "y", LEFT)
    b_right = lax.ppermute(close[0, 1], "y", RIGHT)
    a_right = lax.ppermute(add(close[0, 0], a_right), "y", RIGHT)
    b_left = lax.ppermute(add(far[1, 1], b_left), "y", LEFT)
    swap = (close[1, 0].astype(F32) + a_right.astype(F32) + a_left.astype(F32)).astype(BF16)
    swap = lax.ppermute(swap, "x", XOR[1])
    kept = (close[1, 1].astype(F32) + b_right.astype(F32) + b_left.astype(F32)).astype(BF16)
    even, odd = jnp.where(expert == 0, kept, swap), jnp.where(expert == 0, swap, kept)
    grad_weights = jnp.transpose(jnp.stack([even, odd], axis=0), (2, 1, 0, 3))

    part, away = slot_terms(hs, gps, gate_up, sub)
    part = add(part, lax.ppermute(away, "core", SWAP))
    part = part.reshape((SIDE, 2, tokens, part.shape[1]))
    total = part[0].astype(F32)
    for n, k in enumerate(near):
        total = total + lax.ppermute(part[n + 1], "z", XOR[k]).astype(F32)
    total = total.astype(BF16)
    rows = total[0].astype(F32) + lax.ppermute(total[1], "x", XOR[1]).astype(F32)
    grad_input = rows[:, :width].astype(BF16)
    grad_prob = jnp.sum(jnp.where(hot, rows[:, None, width:], 0.0), axis=2)
    return (grad_input, grad_prob, grad_weights)


def solution(mesh):
    grid = Mesh(mesh.devices.reshape(4, 4, 4, 2), ("y", "x", "z", "core"))
    every = P(("y", "x", "z", "core"), None)
    return jax.shard_map(
        shards,
        mesh=grid,
        in_specs=(every, every, every, every, P(None, None, ("z", "core"), None), P(None, ("z", "core"), None)),
        out_specs=(every, every, P(("y", "x"), None, ("z", "core"), None)),
        check_vma=False,
    )
```

```python
import functools

import jax
import jax.numpy as jnp
from jax import lax
from jax.experimental import pallas as pl
from jax.experimental.pallas import tpu as pltpu
from jax.sharding import Mesh, PartitionSpec as P

F32 = jnp.float32
BF16 = jnp.bfloat16
LANES = 128
SIDE = 4
VMEM = 44 << 20

X_ORDER = ((1, 3, 2), (3, 1, 2))
Z_ORDER = (1, 3, 2)
PAIR = (1, 3)


def plane(step, first):
    pairs = []
    for x in range(SIDE):
        for z in range(SIDE):
            for core in range(2):
                if (core == 0) == first:
                    to = (x ^ X_ORDER[core][step], z)
                else:
                    to = (x, z ^ Z_ORDER[step])
                pairs.append(((x * SIDE + z) * 2 + core, (to[0] * SIDE + to[1]) * 2 + core))
    return pairs


SWAP = [(0, 1), (1, 0)]
Z_MOVE = [[(j, j ^ k) for j in range(SIDE)] for k in Z_ORDER]
X_PAIR = [(x * 2 + c, (x ^ PAIR[c]) * 2 + c) for x in range(SIDE) for c in range(2)]
RING = [(y * 2 + c, ((y + 1 - 2 * c) % SIDE) * 2 + c) for y in range(SIDE) for c in range(2)]


def forward_kernel(width, blocks, cols_ref, *refs):
    row_refs = refs[: 2 * blocks]
    sel_ref, gate_ref, up_ref, down_ref = refs[2 * blocks : 2 * blocks + 4]
    h_ref, gp_ref, xs_ref, ds_ref = refs[2 * blocks + 4 :]
    step = pl.program_id(0)
    half = row_refs[0].shape[0]
    for block in range(blocks):
        pair = row_refs[2 * block : 2 * block + 2]
        rows = slice(2 * half * block, 2 * half * (block + 1))
        x = jnp.concatenate([r[:, :width] for r in pair], axis=0)
        dy = jnp.concatenate([r[:, width : 2 * width] for r in pair], axis=0)
        p = jnp.concatenate([r[:, 2 * width :] for r in pair], axis=0).astype(F32)
        p = jnp.sum(p * sel_ref[...], axis=-1, keepdims=True)
        gate = jnp.dot(x, gate_ref[...], preferred_element_type=F32)
        up = jnp.dot(x, up_ref[...], preferred_element_type=F32)
        back = jnp.dot(dy, down_ref[...], preferred_element_type=F32)
        sig = 1.0 / (1.0 + jnp.exp(-gate))
        act = gate * sig
        hidden = act * up
        hidden_grad = p * back
        h_ref[0, rows] = (hidden_grad * up * (sig * (1.0 + gate * (1.0 - sig)))).astype(BF16)
        h_ref[1, rows] = (hidden_grad * act).astype(BF16)
        h_ref[2, rows] = (p * hidden).astype(BF16)
        term = jnp.sum(hidden * back, axis=-1, keepdims=True) * sel_ref[...]

        @pl.when(step == 0)
        def _():
            gp_ref[rows] = term

        @pl.when(step != 0)
        def _():
            gp_ref[rows] = gp_ref[rows] + term

    @pl.when(step == 0)
    def _():
        for n in range(xs_ref.shape[1] // LANES):
            for piece, ref in enumerate(row_refs):
                rows = slice(half * piece, half * (piece + 1))
                to = slice(n * LANES, (n + 1) * LANES)
                xs_ref[rows, to] = ref[:, pl.ds(pl.multiple_of(cols_ref[n] * LANES, LANES), LANES)]
                ds_ref[rows, to] = ref[:, pl.ds(pl.multiple_of(width + cols_ref[n] * LANES, LANES), LANES)]


def forward(cols, pieces, sel, gate_up, down):
    half, columns = pieces[0].shape
    width, hidden = down.shape
    tokens = len(pieces) * half
    count = cols.shape[0]
    tile = 256
    whole = lambda shape, **kw: pl.BlockSpec(shape, lambda j, cols: (0,) * len(shape), **kw)
    return pl.pallas_call(
        functools.partial(forward_kernel, width, len(pieces) // 2),
        name="forward",
        grid_spec=pltpu.PrefetchScalarGridSpec(
            num_scalar_prefetch=1,
            grid=(hidden // tile,),
            in_specs=[whole((half, columns), pipeline_mode=pl.Buffered(1))] * len(pieces)
            + [
                whole((1, LANES)),
                pl.BlockSpec((None, width, tile), lambda j, cols: (0, 0, j)),
                pl.BlockSpec((None, width, tile), lambda j, cols: (1, 0, j)),
                pl.BlockSpec((width, tile), lambda j, cols: (0, j)),
            ],
            out_specs=[
                pl.BlockSpec((3, tokens, tile), lambda j, cols: (0, 0, j)),
                whole((tokens, LANES)),
                whole((tokens, count * LANES)),
                whole((tokens, count * LANES)),
            ],
        ),
        out_shape=[
            jax.ShapeDtypeStruct((3, tokens, hidden), BF16),
            jax.ShapeDtypeStruct((tokens, LANES), F32),
            jax.ShapeDtypeStruct((tokens, count * LANES), BF16),
            jax.ShapeDtypeStruct((tokens, count * LANES), BF16),
        ],
        compiler_params=pltpu.CompilerParams(vmem_limit_bytes=VMEM),
        cost_estimate=pl.CostEstimate(
            flops=6 * tokens * width * hidden, bytes_accessed=6 * width * hidden, transcendentals=0
        ),
    )(cols, *pieces, sel, gate_up, gate_up, down)


def weight_kernel(x_ref, dy_ref, h_ref, other_ref, own_ref):
    kind = pl.program_id(0)
    contract = (((0,), (0,)), ((), ()))

    def store(rows_ref):
        total = lax.dot_general(rows_ref[...], h_ref[...], contract, preferred_element_type=F32)
        other_ref[...] = total[:LANES].astype(BF16)
        own_ref[...] = total[LANES:].astype(BF16)

    @pl.when(kind < 2)
    def _():
        store(x_ref)

    @pl.when(kind == 2)
    def _():
        store(dy_ref)


def weight_terms(xs, ds, h, start, steps):
    _, tokens, hidden = h.shape
    column = pl.BlockSpec((tokens, 2 * LANES), lambda k, j: (0, start + j))
    out = jax.ShapeDtypeStruct((steps, 3, LANES, hidden), BF16)
    return pl.pallas_call(
        weight_kernel,
        name="weight_terms",
        grid=(3, steps),
        in_specs=[column, column, pl.BlockSpec((None, tokens, hidden), lambda k, j: (k, 0, 0))],
        out_specs=[pl.BlockSpec((None, None, LANES, hidden), lambda k, j: (j, k, 0, 0))] * 2,
        out_shape=[out, out],
        compiler_params=pltpu.CompilerParams(vmem_limit_bytes=VMEM),
        cost_estimate=pl.CostEstimate(
            flops=12 * steps * tokens * LANES * hidden,
            bytes_accessed=6 * tokens * hidden,
            transcendentals=0,
        ),
    )(xs, ds, h)


def slot_rows(core, tokens):
    order = []
    for x in range(2):
        for which in range(2):
            place = 0 if x == 0 else 1 + which
            for z in range(SIDE):
                block, inner = (z, place) if which == core else (place, z)
                order.append(((block * 2 + which) * SIDE + inner) * tokens)
    return order


def slot_kernel(tokens, width, core_ref, h_ref, gp_ref, gate_ref, up_ref, own_ref, pair_ref, rows_ref):
    step = pl.program_id(0)
    half = own_ref.shape[0]

    @pl.when(step == 0)
    def _():
        for core in range(2):

            @pl.when(core_ref[0] == core)
            def _():
                for n, at in enumerate(slot_rows(core, tokens)):
                    to = slice(n * tokens, (n + 1) * tokens)
                    rows_ref[:, to] = h_ref[:, at : at + tokens]
                    out, first = (own_ref, 0) if n * tokens < half else (pair_ref, half)
                    out[n * tokens - first : (n + 1) * tokens - first, width:] = gp_ref[
                        at : at + tokens
                    ].astype(BF16)

    contract = (((1,), (1,)), ((), ()))
    tile = gate_ref.shape[0]
    cols = pl.ds(pl.multiple_of(step * tile, tile), tile)
    total = lax.dot_general(rows_ref[0], gate_ref[...], contract, preferred_element_type=F32)
    total += lax.dot_general(rows_ref[1], up_ref[...], contract, preferred_element_type=F32)
    own_ref[:, cols] = total[:half].astype(BF16)
    pair_ref[:, cols] = total[half:].astype(BF16)


def slot_terms(core, h, gp, gate_up, tokens):
    _, width, hidden = gate_up.shape
    tile = 512
    half = 2 * SIDE * tokens
    out = jax.ShapeDtypeStruct((half, width + LANES), BF16)
    return pl.pallas_call(
        functools.partial(slot_kernel, tokens, width),
        name="slot_terms",
        grid_spec=pltpu.PrefetchScalarGridSpec(
            num_scalar_prefetch=1,
            grid=(width // tile,),
            in_specs=[
                pl.BlockSpec((2,) + h.shape[1:], lambda j, core: (0, 0, 0)),
                pl.BlockSpec(gp.shape, lambda j, core: (0, 0)),
                pl.BlockSpec((None, tile, hidden), lambda j, core: (0, j, 0)),
                pl.BlockSpec((None, tile, hidden), lambda j, core: (1, j, 0)),
            ],
            out_specs=[pl.BlockSpec(out.shape, lambda j, core: (0, 0))] * 2,
            scratch_shapes=[pltpu.VMEM((2, 2 * half, hidden), BF16)],
        ),
        out_shape=[out, out],
        compiler_params=pltpu.CompilerParams(vmem_limit_bytes=VMEM),
        cost_estimate=pl.CostEstimate(
            flops=8 * half * width * hidden, bytes_accessed=4 * width * hidden, transcendentals=0
        ),
    )(core[None].astype(jnp.int32), h, gp, gate_up, gate_up)


def add(*terms):
    total = terms[0].astype(F32)
    for term in terms[1:]:
        total = total + term.astype(F32)
    return total.astype(BF16)


def shards(layer_input, out_grad, routes, probs, gate_up, down_t):
    tokens, width = layer_input.shape
    x, y = lax.axis_index("x"), lax.axis_index("y")
    z, core = lax.axis_index("z"), lax.axis_index("core")
    expert = x % 2
    lane = lax.broadcasted_iota(jnp.int32, (1, LANES), 1)
    sel = (lane == (z * 2 + core) * 2 + expert).astype(F32)

    hot = routes[:, :, None] == lax.broadcasted_iota(jnp.int32, (1, 1, LANES), 2)
    dense = jnp.sum(jnp.where(hot, probs.astype(F32)[:, :, None], 0.0), axis=1).astype(BF16)
    row = jnp.concatenate([layer_input, out_grad, dense], axis=1)

    axes = ("x", "z", "core")
    line = [row] + [lax.ppermute(row, axes, plane(n, True)) for n in range(3)]
    line = jnp.concatenate(line, axis=0)
    mine = [line] + [lax.ppermute(line, axes, plane(n, False)) for n in range(3)]

    gate_up = jnp.where(expert == 0, gate_up[:, :, 0], gate_up[:, :, 1])
    gate_up = jnp.transpose(gate_up, (1, 0, 2))
    down = jnp.where(expert == 0, down_t[:, 0], down_t[:, 1])
    line, gate_up, down = lax.optimization_barrier((line, gate_up, down))
    pieces = []
    for n, piece in enumerate(mine):
        pieces += [piece, lax.ppermute(line if n == 0 else piece, "core", SWAP)]

    cols = []
    pair = x ^ jnp.where(core == 0, PAIR[0], PAIR[1])
    for n in (3, 2, 1, 0):
        base = SIDE * ((y + jnp.where(core == 0, n, SIDE - n)) % SIDE)
        cols += [base + pair, base + x]
    cols = jnp.stack(cols).astype(jnp.int32)
    h, gp, xs, ds = forward(cols, pieces, sel, gate_up, down)

    first = weight_terms(xs, ds, h, 0, 1)
    other = lax.ppermute(first[0][0], ("y", "core"), RING)
    own = lax.ppermute(first[1][0], ("y", "core"), RING)
    rest = weight_terms(xs, ds, h, 1, 3)
    h_late, _ = lax.optimization_barrier((h, rest[0]))
    part, away = slot_terms(core, h_late, gp, gate_up, tokens)

    part = add(part, lax.ppermute(away, ("x", "core"), X_PAIR))
    half = part.shape[0] // 2
    part = add(part[:half], lax.ppermute(part[half:], "core", SWAP))
    part = part.reshape((SIDE, tokens, part.shape[1]))
    total = part[0].astype(F32)
    for n in range(3):
        total = total + lax.ppermute(part[n + 1], "z", Z_MOVE[n]).astype(F32)
    grad_input = total[:, :width].astype(BF16)
    grad_prob = jnp.sum(jnp.where(hot, total[:, None, width:], 0.0), axis=2)

    for n in range(2):
        other = lax.ppermute(add(rest[0][n], other), ("y", "core"), RING)
        own = lax.ppermute(add(rest[1][n], own), ("y", "core"), RING)
    other = lax.ppermute(add(rest[0][2], other), ("x", "core"), X_PAIR)
    own = add(rest[1][2], own)
    even, odd = jnp.where(expert == 0, own, other), jnp.where(expert == 0, other, own)
    grad_weights = jnp.transpose(jnp.stack([even, odd], axis=0), (2, 1, 0, 3))
    return (grad_input, grad_prob, grad_weights)


def solution(mesh):
    grid = Mesh(mesh.devices.reshape(4, 4, 4, 2), ("y", "x", "z", "core"))
    every = P(("y", "x", "z", "core"), None)
    return jax.shard_map(
        shards,
        mesh=grid,
        in_specs=(every, every, every, every, P(None, None, ("z", "core"), None), P(None, ("z", "core"), None)),
        out_specs=(every, every, P(("y", "x"), None, ("z", "core"), None)),
        check_vma=False,
    )
```

```python
import functools

import jax
import jax.numpy as jnp
from jax import lax
from jax.experimental import pallas as pl
from jax.experimental.pallas import tpu as pltpu
from jax.sharding import Mesh, PartitionSpec as P

F32 = jnp.float32
BF16 = jnp.bfloat16
LANES = 128
SIDE = 4
VMEM = 12 << 20
LIGHT = pl.CostEstimate(flops=1 << 20, bytes_accessed=1 << 16, transcendentals=0)

X_ORDER = ((1, 3, 2), (3, 1, 2))
Z_ORDER = (1, 3, 2)
PAIR = (1, 3)
CHUNKS = ((0,), (1, 2, 3))


def plane(step, first):
    pairs = []
    for x in range(SIDE):
        for z in range(SIDE):
            for core in range(2):
                if (core == 0) == first:
                    to = (x ^ X_ORDER[core][step], z)
                else:
                    to = (x, z ^ Z_ORDER[step])
                pairs.append(((x * SIDE + z) * 2 + core, (to[0] * SIDE + to[1]) * 2 + core))
    return pairs


SWAP = [(0, 1), (1, 0)]
Z_MOVE = [[(j, j ^ k) for j in range(SIDE)] for k in Z_ORDER]
X_PAIR = [(x * 2 + c, (x ^ PAIR[c]) * 2 + c) for x in range(SIDE) for c in range(2)]
RING = [(y * 2 + c, ((y + 1 - 2 * c) % SIDE) * 2 + c) for y in range(SIDE) for c in range(2)]


def hold_kernel(place_ref, gate_up_ref, down_ref, held_ref, sem):
    expert = place_ref[1]
    sources = (gate_up_ref.at[0, expert], gate_up_ref.at[1, expert], down_ref.at[expert])
    copies = [pltpu.make_async_copy(source, held_ref.at[n], sem.at[n]) for n, source in enumerate(sources)]
    for copy in copies:
        copy.start()
    for copy in copies:
        copy.wait()


def forward_rows(row_refs, place_ref, sel_ref, weights_ref, h_ref, gp_ref):
    half = row_refs[0].shape[0]
    _, width, hidden = weights_ref.shape
    tile = 256
    gp_ref[...] = jnp.zeros_like(gp_ref)

    def step(j, carry):
        cols = pl.ds(pl.multiple_of(j * tile, tile), tile)
        for block in range(len(row_refs) // 2):
            pair = row_refs[2 * block : 2 * block + 2]
            rows = slice(2 * half * block, 2 * half * (block + 1))
            x = jnp.concatenate([r[:, :width] for r in pair], axis=0)
            dy = jnp.concatenate([r[:, width : 2 * width] for r in pair], axis=0)
            p = jnp.concatenate([r[:, 2 * width :] for r in pair], axis=0).astype(F32)
            p = jnp.sum(p * sel_ref[...], axis=-1, keepdims=True)
            gate = jnp.dot(x, weights_ref[0, :, cols], preferred_element_type=F32)
            up = jnp.dot(x, weights_ref[1, :, cols], preferred_element_type=F32)
            back = jnp.dot(dy, weights_ref[2, :, cols], preferred_element_type=F32)
            sig = 1.0 / (1.0 + jnp.exp(-gate))
            act = gate * sig
            hid = act * up
            hidden_grad = p * back
            h_ref[0, rows, cols] = (hidden_grad * up * (sig * (1.0 + gate * (1.0 - sig)))).astype(BF16)
            h_ref[1, rows, cols] = (hidden_grad * act).astype(BF16)
            h_ref[2, rows, cols] = (p * hid).astype(BF16)
            term = hid * back
            gp_ref[rows] += term[:, :LANES] + term[:, LANES:]
        return carry

    lax.fori_loop(0, hidden // tile, step, 0)


def weight_rows(width, start, cols_ref, row_refs, h_refs, other_ref, own_ref, rows_ref):
    half = row_refs[0].shape[0]

    def step(r, carry):
        for n in range(2):
            for m in range(2):
                at = pl.ds(pl.multiple_of(cols_ref[2 + 2 * (start + r) + m] * LANES + n * width, LANES), LANES)
                for piece, ref in enumerate(row_refs):
                    rows_ref[n, m * LANES : (m + 1) * LANES, half * piece : half * (piece + 1)] = ref[:, at].T
        for kind in range(3):
            total = None
            first = 0
            for h in h_refs:
                span = slice(first, first + h.shape[1])
                first += h.shape[1]
                term = jnp.dot(rows_ref[kind // 2, :, span], h[kind], preferred_element_type=F32)
                total = term if total is None else total + term
            other_ref[r, kind] = total[:LANES].astype(BF16)
            own_ref[r, kind] = total[LANES:].astype(BF16)
        return carry

    lax.fori_loop(0, other_ref.shape[0], step, 0)


def early_kernel(place_ref, sel_ref, weights_ref, *refs):
    *row_refs, h_ref, gp_ref = refs
    forward_rows(row_refs, place_ref, sel_ref, weights_ref, h_ref, gp_ref)


def late_kernel(old, count, place_ref, sel_ref, weights_ref, old_h_ref, *refs):
    row_refs, (h_ref, gp_ref, other_ref, own_ref, rows_ref) = refs[:count], refs[count:]
    forward_rows(row_refs[old:], place_ref, sel_ref, weights_ref, h_ref, gp_ref)
    cols = place_ref
    weight_rows(weights_ref.shape[1], 0, cols, row_refs, (old_h_ref, h_ref), other_ref, own_ref, rows_ref)


def rest_kernel(count, width, place_ref, *refs):
    row_refs, h_refs, (other_ref, own_ref, rows_ref) = refs[:count], refs[count:-3], refs[-3:]
    cols = place_ref
    weight_rows(width, 1, cols, row_refs, h_refs, other_ref, own_ref, rows_ref)


def on_chip(kernel, name, args, outs, scratch=(), far=0):
    vmem = pl.BlockSpec(memory_space=pltpu.VMEM)
    return pl.pallas_call(
        kernel,
        name=name,
        in_specs=[pl.BlockSpec(memory_space=pltpu.SMEM)]
        + [pl.BlockSpec(memory_space=pl.ANY)] * far
        + [vmem] * (len(args) - 1 - far),
        out_specs=[vmem] * len(outs),
        out_shape=[jax.ShapeDtypeStruct(*out) for out in outs],
        scratch_shapes=list(scratch),
        compiler_params=pltpu.CompilerParams(vmem_limit_bytes=VMEM),
        cost_estimate=LIGHT,
    )(*args)


def slot_rows(core, tokens):
    order = []
    for x in range(2):
        for which in range(2):
            place = 0 if x == 0 else 1 + which
            for z in range(SIDE):
                block, inner = (z, place) if which == core else (place, z)
                chunk = [block in blocks for blocks in CHUNKS].index(True)
                at = CHUNKS[chunk].index(block)
                order.append((chunk, ((at * 2 + which) * SIDE + inner) * tokens))
    return order


def slot_kernel(tokens, chunks, place_ref, sel_ref, weights_ref, *refs):
    hs, gps = refs[:chunks], refs[chunks : 2 * chunks]
    own_ref, pair_ref, rows_ref = refs[2 * chunks :]
    _, width, hidden = weights_ref.shape
    half = own_ref.shape[0]
    for core in range(2):

        @pl.when(place_ref[0] == core)
        def _():
            for n, (chunk, at) in enumerate(slot_rows(core, tokens)):
                to = slice(n * tokens, (n + 1) * tokens)
                rows_ref[:, to] = hs[chunk][:2, at : at + tokens]
                out, first = (own_ref, 0) if n * tokens < half else (pair_ref, half)
                gp = jnp.sum(gps[chunk][at : at + tokens], axis=-1, keepdims=True) * sel_ref[...]
                out[n * tokens - first : (n + 1) * tokens - first, width:] = gp.astype(BF16)

    contract = (((1,), (1,)), ((), ()))
    tile = 256

    def step(j, carry):
        cols = pl.ds(pl.multiple_of(j * tile, tile), tile)
        total = lax.dot_general(
            rows_ref[0], weights_ref[0, cols], contract, preferred_element_type=F32
        ) + lax.dot_general(rows_ref[1], weights_ref[1, cols], contract, preferred_element_type=F32)
        own_ref[:, cols] = total[:half].astype(BF16)
        pair_ref[:, cols] = total[half:].astype(BF16)
        return carry

    lax.fori_loop(0, width // tile, step, 0)


def add(*terms):
    total = terms[0].astype(F32)
    for term in terms[1:]:
        total = total + term.astype(F32)
    return total.astype(BF16)


def shards(layer_input, out_grad, routes, probs, gate_up, down_t):
    tokens, width = layer_input.shape
    x, y = lax.axis_index("x"), lax.axis_index("y")
    z, core = lax.axis_index("z"), lax.axis_index("core")
    expert = x % 2
    lane = lax.broadcasted_iota(jnp.int32, (1, LANES), 1)
    sel = (lane == (z * 2 + core) * 2 + expert).astype(F32)

    hot = routes[:, :, None] == lax.broadcasted_iota(jnp.int32, (1, 1, LANES), 2)
    dense = jnp.sum(jnp.where(hot, probs.astype(F32)[:, :, None], 0.0), axis=1).astype(BF16)
    row = jnp.concatenate([layer_input, out_grad, dense], axis=1)

    axes = ("x", "z", "core")
    down = jnp.transpose(down_t, (1, 0, 2))
    line = [row] + [lax.ppermute(row, axes, plane(n, True)) for n in range(3)]
    line = jnp.concatenate(line, axis=0)
    line, down = lax.optimization_barrier((line, down))
    mine = [line] + [lax.ppermute(line, axes, plane(n, False)) for n in range(3)]

    gate_up = jnp.transpose(gate_up, (1, 2, 0, 3))

    cols = []
    pair = x ^ jnp.where(core == 0, PAIR[0], PAIR[1])
    for n in (3, 2, 1, 0):
        base = SIDE * ((y + jnp.where(core == 0, n, SIDE - n)) % SIDE)
        cols += [base + pair, base + x]
    place = jnp.stack([core, expert] + cols).astype(jnp.int32)
    gate_up = pltpu.with_memory_space_constraint(gate_up, pltpu.HBM)
    down = pltpu.with_memory_space_constraint(down, pltpu.HBM)
    hidden = down.shape[2]
    (weights,) = on_chip(
        hold_kernel,
        "hold",
        (place, gate_up, down),
        [((3, width, hidden), BF16)],
        [pltpu.SemaphoreType.DMA((3,))],
        2,
    )
    swap = lambda piece: [piece, lax.ppermute(piece, "core", SWAP)]
    pieces = swap(line)
    early = 2 * line.shape[0]
    h0, gp0 = on_chip(
        early_kernel,
        "forward",
        (place, sel, weights, *pieces),
        [((3, early, hidden), BF16), ((early, LANES), F32)],
    )
    *mine[1:3], h0 = lax.optimization_barrier((*mine[1:3], h0))
    for piece in mine[1:]:
        pieces += swap(piece)
    late = 3 * early
    moving = lambda steps: ((steps, 3, LANES, hidden), BF16)
    turned = pltpu.VMEM((2, 2 * LANES, early + late), BF16)
    h1, gp1, other, own = on_chip(
        functools.partial(late_kernel, 2, len(pieces)),
        "forward_and_first",
        (place, sel, weights, h0, *pieces),
        [((3, late, hidden), BF16), ((late, LANES), F32), moving(1), moving(1)],
        [turned],
    )

    ring = lambda rows: lax.ppermute(rows, ("y", "core"), RING)
    other, own = ring(other[0]), ring(own[0])
    rest = on_chip(
        functools.partial(rest_kernel, len(pieces), width),
        "weight_terms",
        (place, *pieces, h0, h1),
        [moving(3), moving(3)],
        [turned],
    )
    other = add(rest[0][0], other)
    other, h1 = lax.optimization_barrier((other, h1))
    other, own = ring(other), ring(add(rest[1][0], own))
    half = 2 * SIDE * tokens
    rows = ((half, width + LANES), BF16)
    part, away = on_chip(
        functools.partial(slot_kernel, tokens, 2),
        "slot_terms",
        (place, sel, weights, h0, h1, gp0, gp1),
        [rows, rows],
        [pltpu.VMEM((2, 2 * half, hidden), BF16)],
    )

    part = add(part, lax.ppermute(away, ("x", "core"), X_PAIR))
    half = part.shape[0] // 2
    part = add(part[:half], lax.ppermute(part[half:], "core", SWAP))
    part = part.reshape((SIDE, tokens, part.shape[1]))
    total = part[0].astype(F32)
    for n in range(3):
        total = total + lax.ppermute(part[n + 1], "z", Z_MOVE[n]).astype(F32)
    grad_input = total[:, :width].astype(BF16)
    grad_prob = jnp.sum(jnp.where(hot, total[:, None, width:], 0.0), axis=2)

    other, own = ring(add(rest[0][1], other)), ring(add(rest[1][1], own))
    other = lax.ppermute(add(rest[0][2], other), ("x", "core"), X_PAIR)
    own = add(rest[1][2], own)
    even, odd = jnp.where(expert == 0, own, other), jnp.where(expert == 0, other, own)
    grad_weights = jnp.transpose(jnp.stack([even, odd], axis=0), (2, 1, 0, 3))
    return (grad_input, grad_prob, grad_weights)


def solution(mesh):
    grid = Mesh(mesh.devices.reshape(4, 4, 4, 2), ("y", "x", "z", "core"))
    every = P(("y", "x", "z", "core"), None)
    return jax.shard_map(
        shards,
        mesh=grid,
        in_specs=(every, every, every, every, P(None, None, ("z", "core"), None), P(None, ("z", "core"), None)),
        out_specs=(every, every, P(("y", "x"), None, ("z", "core"), None)),
        check_vma=False,
    )
```

```python
import functools

import jax
import jax.numpy as jnp
from jax import lax
from jax.experimental import pallas as pl
from jax.experimental.pallas import tpu as pltpu
from jax.sharding import Mesh, PartitionSpec as P

F32 = jnp.float32
BF16 = jnp.bfloat16
LANES = 128
SIDE = 4
VMEM = 12 << 20
LIGHT = pl.CostEstimate(flops=1 << 20, bytes_accessed=1 << 16, transcendentals=0)

X_ORDER = ((1, 3, 2), (3, 1, 2))
Z_ORDER = (1, 3, 2)
PAIR = (1, 3)


def plane(step, first):
    pairs = []
    for x in range(SIDE):
        for z in range(SIDE):
            for core in range(2):
                if (core == 0) == first:
                    to = (x ^ X_ORDER[core][step], z)
                else:
                    to = (x, z ^ Z_ORDER[step])
                pairs.append(((x * SIDE + z) * 2 + core, (to[0] * SIDE + to[1]) * 2 + core))
    return pairs


SWAP = [(0, 1), (1, 0)]
Z_MOVE = [[(j, j ^ k) for j in range(SIDE)] for k in Z_ORDER]
X_PAIR = [(x * 2 + c, (x ^ PAIR[c]) * 2 + c) for x in range(SIDE) for c in range(2)]
RING = [(y * 2 + c, ((y + 1 - 2 * c) % SIDE) * 2 + c) for y in range(SIDE) for c in range(2)]


def hold_kernel(place_ref, gate_up_ref, down_ref, held_ref, sem):
    expert = place_ref[1]
    sources = (gate_up_ref.at[0, expert], gate_up_ref.at[1, expert], down_ref.at[expert])
    copies = [pltpu.make_async_copy(source, held_ref.at[n], sem.at[n]) for n, source in enumerate(sources)]
    for copy in copies:
        copy.start()
    for copy in copies:
        copy.wait()


def forward_rows(row_refs, size, sel_ref, weights_ref, h_ref, gp_ref):
    half = row_refs[0].shape[0]
    _, width, hidden = weights_ref.shape
    tile = 256
    gp_ref[...] = jnp.zeros_like(gp_ref)

    def step(j, carry):
        cols = pl.ds(pl.multiple_of(j * tile, tile), tile)
        for first in range(0, len(row_refs), size):
            pair = row_refs[first : first + size]
            rows = slice(half * first, half * (first + size))
            x = jnp.concatenate([r[:, :width] for r in pair], axis=0)
            dy = jnp.concatenate([r[:, width : 2 * width] for r in pair], axis=0)
            p = jnp.concatenate([r[:, 2 * width :] for r in pair], axis=0).astype(F32)
            p = jnp.sum(p * sel_ref[...], axis=-1, keepdims=True)
            gate = jnp.dot(x, weights_ref[0, :, cols], preferred_element_type=F32)
            up = jnp.dot(x, weights_ref[1, :, cols], preferred_element_type=F32)
            back = jnp.dot(dy, weights_ref[2, :, cols], preferred_element_type=F32)
            sig = 1.0 / (1.0 + jnp.exp(-gate))
            act = gate * sig
            hid = act * up
            hidden_grad = p * back
            h_ref[0, rows, cols] = (hidden_grad * up * (sig * (1.0 + gate * (1.0 - sig)))).astype(BF16)
            h_ref[1, rows, cols] = (hidden_grad * act).astype(BF16)
            h_ref[2, rows, cols] = (p * hid).astype(BF16)
            term = hid * back
            gp_ref[rows] += term[:, :LANES] + term[:, LANES:]
        return carry

    lax.fori_loop(0, hidden // tile, step, 0)


def weight_rows(width, start, cols_ref, row_refs, h_refs, other_ref, own_ref, rows_ref):
    half = row_refs[0].shape[0]

    def step(r, carry):
        for n in range(2):
            for m in range(2):
                at = pl.ds(pl.multiple_of(cols_ref[2 + 2 * (start + r) + m] * LANES + n * width, LANES), LANES)
                for piece, ref in enumerate(row_refs):
                    rows_ref[n, m * LANES : (m + 1) * LANES, half * piece : half * (piece + 1)] = ref[:, at].T
        for kind in range(3):
            total = None
            first = 0
            for h in h_refs:
                span = slice(first, first + h.shape[1])
                first += h.shape[1]
                term = jnp.dot(rows_ref[kind // 2, :, span], h[kind], preferred_element_type=F32)
                total = term if total is None else total + term
            other_ref[r, kind] = total[:LANES].astype(BF16)
            own_ref[r, kind] = total[LANES:].astype(BF16)
        return carry

    lax.fori_loop(0, other_ref.shape[0], step, 0)


def early_kernel(place_ref, sel_ref, weights_ref, *refs):
    *row_refs, h_ref, gp_ref = refs
    forward_rows(row_refs, len(row_refs), sel_ref, weights_ref, h_ref, gp_ref)


def late_kernel(old, place_ref, sel_ref, weights_ref, *refs):
    h_refs, refs = refs[: len(old)], refs[len(old) :]
    row_refs, (h_ref, gp_ref, other_ref, own_ref, turned_ref) = refs[:-5], refs[-5:]
    last = row_refs[sum(old) :]
    forward_rows(last, len(last), sel_ref, weights_ref, h_ref, gp_ref)
    hs = (*h_refs, h_ref)
    weight_rows(weights_ref.shape[1], 0, place_ref, row_refs, hs, other_ref, own_ref, turned_ref)


def rest_kernel(count, width, place_ref, *refs):
    row_refs, h_refs, (other_ref, own_ref, rows_ref) = refs[:count], refs[count:-3], refs[-3:]
    weight_rows(width, 2, place_ref, row_refs, h_refs, other_ref, own_ref, rows_ref)


def on_chip(kernel, name, args, outs, scratch=(), far=0):
    vmem = pl.BlockSpec(memory_space=pltpu.VMEM)
    return pl.pallas_call(
        kernel,
        name=name,
        in_specs=[pl.BlockSpec(memory_space=pltpu.SMEM)]
        + [pl.BlockSpec(memory_space=pl.ANY)] * far
        + [vmem] * (len(args) - 1 - far),
        out_specs=[vmem] * len(outs),
        out_shape=[jax.ShapeDtypeStruct(*out) for out in outs],
        scratch_shapes=list(scratch),
        compiler_params=pltpu.CompilerParams(vmem_limit_bytes=VMEM),
        cost_estimate=LIGHT,
    )(*args)


def slot_rows(core, tokens):
    order = []
    for x in range(2):
        for which in range(2):
            place = 0 if x == 0 else 1 + which
            for z in range(SIDE):
                block, inner = (z, place) if which == core else (place, z)
                chunk, at = (0, which) if block == 0 else (1 + which, block - 1)
                order.append((chunk, (at * SIDE + inner) * tokens))
    return order


def slot_kernel(tokens, chunks, place_ref, sel_ref, weights_ref, *refs):
    hs, gps, refs = refs[:chunks], refs[chunks : 2 * chunks], refs[2 * chunks :]
    row_refs, (next_other_ref, next_own_ref, own_ref, pair_ref, turned_ref, rows_ref) = refs[:-6], refs[-6:]
    _, width, hidden = weights_ref.shape
    weight_rows(width, 1, place_ref, row_refs, hs, next_other_ref, next_own_ref, turned_ref)
    half = own_ref.shape[0]
    for core in range(2):

        @pl.when(place_ref[0] == core)
        def _():
            for n, (chunk, at) in enumerate(slot_rows(core, tokens)):
                to = slice(n * tokens, (n + 1) * tokens)
                rows_ref[:, to] = hs[chunk][:2, at : at + tokens]
                out, first = (own_ref, 0) if n * tokens < half else (pair_ref, half)
                gp = jnp.sum(gps[chunk][at : at + tokens], axis=-1, keepdims=True) * sel_ref[...]
                out[n * tokens - first : (n + 1) * tokens - first, width:] = gp.astype(BF16)

    contract = (((1,), (1,)), ((), ()))
    tile = 256

    def step(j, carry):
        cols = pl.ds(pl.multiple_of(j * tile, tile), tile)
        total = lax.dot_general(
            rows_ref[0], weights_ref[0, cols], contract, preferred_element_type=F32
        ) + lax.dot_general(rows_ref[1], weights_ref[1, cols], contract, preferred_element_type=F32)
        own_ref[:, cols] = total[:half].astype(BF16)
        pair_ref[:, cols] = total[half:].astype(BF16)
        return carry

    lax.fori_loop(0, width // tile, step, 0)


def add(*terms):
    total = terms[0].astype(F32)
    for term in terms[1:]:
        total = total + term.astype(F32)
    return total.astype(BF16)


def shards(layer_input, out_grad, routes, probs, gate_up, down_t):
    tokens, width = layer_input.shape
    x, y = lax.axis_index("x"), lax.axis_index("y")
    z, core = lax.axis_index("z"), lax.axis_index("core")
    expert = x % 2
    lane = lax.broadcasted_iota(jnp.int32, (1, LANES), 1)
    sel = (lane == (z * 2 + core) * 2 + expert).astype(F32)

    hot = routes[:, :, None] == lax.broadcasted_iota(jnp.int32, (1, 1, LANES), 2)
    dense = jnp.sum(jnp.where(hot, probs.astype(F32)[:, :, None], 0.0), axis=1).astype(BF16)
    row = jnp.concatenate([layer_input, out_grad, dense], axis=1)

    axes = ("x", "z", "core")
    down = jnp.transpose(down_t, (1, 0, 2))
    line = [row] + [lax.ppermute(row, axes, plane(n, True)) for n in range(3)]
    line = jnp.concatenate(line, axis=0)
    line, down = lax.optimization_barrier((line, down))
    mine = [line] + [lax.ppermute(line, axes, plane(n, False)) for n in range(3)]

    gate_up = jnp.transpose(gate_up, (1, 2, 0, 3))

    cols = []
    pair = x ^ jnp.where(core == 0, PAIR[0], PAIR[1])
    for n in (3, 2, 1, 0):
        base = SIDE * ((y + jnp.where(core == 0, n, SIDE - n)) % SIDE)
        cols += [base + pair, base + x]
    place = jnp.stack([core, expert] + cols).astype(jnp.int32)
    gate_up = pltpu.with_memory_space_constraint(gate_up, pltpu.HBM)
    down = pltpu.with_memory_space_constraint(down, pltpu.HBM)
    hidden = down.shape[2]
    (weights,) = on_chip(
        hold_kernel,
        "hold",
        (place, gate_up, down),
        [((3, width, hidden), BF16)],
        [pltpu.SemaphoreType.DMA((3,))],
        2,
    )
    swap = lambda piece: [piece, lax.ppermute(piece, "core", SWAP)]
    pieces = swap(line)
    span = line.shape[0]
    forwarded = lambda count: [((3, count * span, hidden), BF16), ((count * span, LANES), F32)]
    h0, gp0 = on_chip(early_kernel, "forward", (place, sel, weights, *pieces), forwarded(2))
    *mine[1:], h0 = lax.optimization_barrier((*mine[1:], h0))
    others = [swap(piece)[1] for piece in mine[1:]]
    h1, gp1 = on_chip(early_kernel, "forward_mine", (place, sel, weights, *mine[1:]), forwarded(3))
    pieces += mine[1:] + others
    moving = lambda steps: ((steps, 3, LANES, hidden), BF16)
    turned = pltpu.VMEM((2, 2 * LANES, len(pieces) * span), BF16)
    h2, gp2, other, own = on_chip(
        functools.partial(late_kernel, (2, 3)),
        "forward_and_first",
        (place, sel, weights, h0, h1, *pieces),
        forwarded(3) + [moving(1)] * 2,
        [turned],
    )

    ring = lambda rows: lax.ppermute(rows, ("y", "core"), RING)
    other, own = ring(other[0]), ring(own[0])
    half = 2 * SIDE * tokens
    rows = ((half, width + LANES), BF16)
    other_next, own_next, part, away = on_chip(
        functools.partial(slot_kernel, tokens, 3),
        "second_and_slots",
        (place, sel, weights, h0, h1, h2, gp0, gp1, gp2, *pieces),
        [moving(1), moving(1), rows, rows],
        [turned, pltpu.VMEM((2, 2 * half, hidden), BF16)],
    )
    other, h2 = lax.optimization_barrier((add(other_next[0], other), h2))
    other = ring(other)
    rest = on_chip(
        functools.partial(rest_kernel, len(pieces), width),
        "weight_terms",
        (place, *pieces, h0, h1, h2),
        [moving(2), moving(2)],
        [turned],
    )
    own, rest = lax.optimization_barrier((own, rest))
    own = ring(add(own_next[0], own))

    away = lax.ppermute(away, ("x", "core"), X_PAIR)
    other, away = lax.optimization_barrier((add(rest[0][0], other), away))
    part = add(part, away)
    half = part.shape[0] // 2
    part = add(part[:half], lax.ppermute(part[half:], "core", SWAP))
    part = part.reshape((SIDE, tokens, part.shape[1]))
    total = part[0].astype(F32)
    for n in range(3):
        total = total + lax.ppermute(part[n + 1], "z", Z_MOVE[n]).astype(F32)
    grad_input = total[:, :width].astype(BF16)
    grad_prob = jnp.sum(jnp.where(hot, total[:, None, width:], 0.0), axis=2)

    other, own = ring(other), ring(add(rest[1][0], own))
    other = lax.ppermute(add(rest[0][1], other), ("x", "core"), X_PAIR)
    own = add(rest[1][1], own)
    even, odd = jnp.where(expert == 0, own, other), jnp.where(expert == 0, other, own)
    grad_weights = jnp.transpose(jnp.stack([even, odd], axis=0), (2, 1, 0, 3))
    return (grad_input, grad_prob, grad_weights)


def solution(mesh):
    grid = Mesh(mesh.devices.reshape(4, 4, 4, 2), ("y", "x", "z", "core"))
    every = P(("y", "x", "z", "core"), None)
    return jax.shard_map(
        shards,
        mesh=grid,
        in_specs=(every, every, every, every, P(None, None, ("z", "core"), None), P(None, ("z", "core"), None)),
        out_specs=(every, every, P(("y", "x"), None, ("z", "core"), None)),
        check_vma=False,
    )
```

```python
import functools

import jax
import jax.numpy as jnp
from jax import lax
from jax.experimental import pallas as pl
from jax.experimental.pallas import tpu as pltpu
from jax.sharding import Mesh, PartitionSpec as P

F32 = jnp.float32
BF16 = jnp.bfloat16
LANES = 128
SIDE = 4
VMEM = 12 << 20
LIGHT = pl.CostEstimate(flops=1 << 20, bytes_accessed=1 << 16, transcendentals=0)

X_ORDER = ((1, 3, 2), (3, 1, 2))
Z_ORDER = (1, 3, 2)
PAIR = (1, 3)


def plane(step, first):
    pairs = []
    for x in range(SIDE):
        for z in range(SIDE):
            for core in range(2):
                if (core == 0) == first:
                    to = (x ^ X_ORDER[core][step], z)
                else:
                    to = (x, z ^ Z_ORDER[step])
                pairs.append(((x * SIDE + z) * 2 + core, (to[0] * SIDE + to[1]) * 2 + core))
    return pairs


SWAP = [(0, 1), (1, 0)]
Z_MOVE = [[(j, j ^ k) for j in range(SIDE)] for k in Z_ORDER]
X_PAIR = [(x * 2 + c, (x ^ PAIR[c]) * 2 + c) for x in range(SIDE) for c in range(2)]
RING = [(y * 2 + c, ((y + 1 - 2 * c) % SIDE) * 2 + c) for y in range(SIDE) for c in range(2)]


def hold_kernel(place_ref, gate_up_ref, down_ref, held_ref, sem):
    expert = place_ref[1]
    sources = (gate_up_ref.at[0, expert], gate_up_ref.at[1, expert], down_ref.at[expert])
    copies = [pltpu.make_async_copy(source, held_ref.at[n], sem.at[n]) for n, source in enumerate(sources)]
    for copy in copies:
        copy.start()
    for copy in copies:
        copy.wait()


def forward_rows(row_refs, size, sel_ref, weights_ref, h_ref, gp_ref):
    half = row_refs[0].shape[0]
    _, width, hidden = weights_ref.shape
    tile = 256
    gp_ref[...] = jnp.zeros_like(gp_ref)

    def step(j, carry):
        cols = pl.ds(pl.multiple_of(j * tile, tile), tile)
        for first in range(0, len(row_refs), size):
            pair = row_refs[first : first + size]
            rows = slice(half * first, half * (first + size))
            x = jnp.concatenate([r[:, :width] for r in pair], axis=0)
            dy = jnp.concatenate([r[:, width : 2 * width] for r in pair], axis=0)
            p = jnp.concatenate([r[:, 2 * width :] for r in pair], axis=0).astype(F32)
            p = jnp.sum(p * sel_ref[...], axis=-1, keepdims=True)
            gate = jnp.dot(x, weights_ref[0, :, cols], preferred_element_type=F32)
            up = jnp.dot(x, weights_ref[1, :, cols], preferred_element_type=F32)
            back = jnp.dot(dy, weights_ref[2, :, cols], preferred_element_type=F32)
            sig = 1.0 / (1.0 + jnp.exp(-gate))
            act = gate * sig
            hid = act * up
            hidden_grad = p * back
            h_ref[0, rows, cols] = (hidden_grad * up * (sig * (1.0 + gate * (1.0 - sig)))).astype(BF16)
            h_ref[1, rows, cols] = (hidden_grad * act).astype(BF16)
            h_ref[2, rows, cols] = (p * hid).astype(BF16)
            term = hid * back
            gp_ref[rows] += term[:, :LANES] + term[:, LANES:]
        return carry

    lax.fori_loop(0, hidden // tile, step, 0)


def weight_rows(width, start, cols_ref, row_refs, h_refs, other_ref, own_ref, rows_ref):
    half = row_refs[0].shape[0]

    def step(r, carry):
        for n in range(2):
            for m in range(2):
                at = pl.ds(pl.multiple_of(cols_ref[2 + 2 * (start + r) + m] * LANES + n * width, LANES), LANES)
                for piece, ref in enumerate(row_refs):
                    rows_ref[n, m * LANES : (m + 1) * LANES, half * piece : half * (piece + 1)] = ref[:, at].T
        for kind in range(3):
            total = None
            first = 0
            for h in h_refs:
                span = slice(first, first + h.shape[1])
                first += h.shape[1]
                term = jnp.dot(rows_ref[kind // 2, :, span], h[kind], preferred_element_type=F32)
                total = term if total is None else total + term
            other_ref[r, kind] = total[:LANES].astype(BF16)
            own_ref[r, kind] = total[LANES:].astype(BF16)
        return carry

    lax.fori_loop(0, other_ref.shape[0], step, 0)


def early_kernel(place_ref, sel_ref, weights_ref, *refs):
    *row_refs, h_ref, gp_ref = refs
    forward_rows(row_refs, len(row_refs), sel_ref, weights_ref, h_ref, gp_ref)


def late_kernel(old, place_ref, sel_ref, weights_ref, *refs):
    h_refs, refs = refs[: len(old)], refs[len(old) :]
    row_refs, (h_ref, gp_ref, other_ref, own_ref, turned_ref) = refs[:-5], refs[-5:]
    last = row_refs[sum(old) :]
    forward_rows(last, len(last), sel_ref, weights_ref, h_ref, gp_ref)
    hs = (*h_refs, h_ref)
    weight_rows(weights_ref.shape[1], 0, place_ref, row_refs, hs, other_ref, own_ref, turned_ref)


def rest_kernel(count, width, place_ref, *refs):
    row_refs, h_refs, (other_ref, own_ref, rows_ref) = refs[:count], refs[count:-3], refs[-3:]
    weight_rows(width, 2, place_ref, row_refs, h_refs, other_ref, own_ref, rows_ref)


def on_chip(kernel, name, args, outs, scratch=(), far=0):
    vmem = pl.BlockSpec(memory_space=pltpu.VMEM)
    return pl.pallas_call(
        kernel,
        name=name,
        in_specs=[pl.BlockSpec(memory_space=pltpu.SMEM)]
        + [pl.BlockSpec(memory_space=pl.ANY)] * far
        + [vmem] * (len(args) - 1 - far),
        out_specs=[vmem] * len(outs),
        out_shape=[jax.ShapeDtypeStruct(*out) for out in outs],
        scratch_shapes=list(scratch),
        compiler_params=pltpu.CompilerParams(vmem_limit_bytes=VMEM),
        cost_estimate=LIGHT,
    )(*args)


def slot_rows(core, tokens):
    order = []
    for x in range(2):
        for which in range(2):
            place = 0 if x == 0 else 1 + which
            for z in range(SIDE):
                block, inner = (z, place) if which == core else (place, z)
                if block == 0 or which == 0 and block == 1:
                    chunk, at = 0, which + 2 * block
                else:
                    chunk, at = (2, block - 1) if which else (1, block - 2)
                order.append((chunk, (at * SIDE + inner) * tokens))
    return order


def slot_kernel(tokens, chunks, place_ref, sel_ref, weights_ref, *refs):
    hs, gps, refs = refs[:chunks], refs[chunks : 2 * chunks], refs[2 * chunks :]
    row_refs, (next_other_ref, next_own_ref, own_ref, pair_ref, turned_ref, rows_ref) = refs[:-6], refs[-6:]
    _, width, hidden = weights_ref.shape
    weight_rows(width, 1, place_ref, row_refs, hs, next_other_ref, next_own_ref, turned_ref)
    half = own_ref.shape[0]
    for core in range(2):

        @pl.when(place_ref[0] == core)
        def _():
            for n, (chunk, at) in enumerate(slot_rows(core, tokens)):
                to = slice(n * tokens, (n + 1) * tokens)
                rows_ref[:, to] = hs[chunk][:2, at : at + tokens]
                out, first = (own_ref, 0) if n * tokens < half else (pair_ref, half)
                gp = jnp.sum(gps[chunk][at : at + tokens], axis=-1, keepdims=True) * sel_ref[...]
                out[n * tokens - first : (n + 1) * tokens - first, width:] = gp.astype(BF16)

    contract = (((1,), (1,)), ((), ()))
    tile = 256

    def step(j, carry):
        cols = pl.ds(pl.multiple_of(j * tile, tile), tile)
        total = lax.dot_general(
            rows_ref[0], weights_ref[0, cols], contract, preferred_element_type=F32
        ) + lax.dot_general(rows_ref[1], weights_ref[1, cols], contract, preferred_element_type=F32)
        own_ref[:, cols] = total[:half].astype(BF16)
        pair_ref[:, cols] = total[half:].astype(BF16)
        return carry

    lax.fori_loop(0, width // tile, step, 0)


def add(*terms):
    total = terms[0].astype(F32)
    for term in terms[1:]:
        total = total + term.astype(F32)
    return total.astype(BF16)


def shards(layer_input, out_grad, routes, probs, gate_up, down_t):
    tokens, width = layer_input.shape
    x, y = lax.axis_index("x"), lax.axis_index("y")
    z, core = lax.axis_index("z"), lax.axis_index("core")
    expert = x % 2
    lane = lax.broadcasted_iota(jnp.int32, (1, LANES), 1)
    sel = (lane == (z * 2 + core) * 2 + expert).astype(F32)

    hot = routes[:, :, None] == lax.broadcasted_iota(jnp.int32, (1, 1, LANES), 2)
    dense = jnp.sum(jnp.where(hot, probs.astype(F32)[:, :, None], 0.0), axis=1).astype(BF16)
    row = jnp.concatenate([layer_input, out_grad, dense], axis=1)

    axes = ("x", "z", "core")
    down = jnp.transpose(down_t, (1, 0, 2))
    line = [row] + [lax.ppermute(row, axes, plane(n, True)) for n in range(3)]
    line = jnp.concatenate(line, axis=0)
    line, down = lax.optimization_barrier((line, down))
    mine = [line] + [lax.ppermute(line, axes, plane(n, False)) for n in range(3)]

    gate_up = jnp.transpose(gate_up, (1, 2, 0, 3))

    cols = []
    pair = x ^ jnp.where(core == 0, PAIR[0], PAIR[1])
    for n in (3, 2, 1, 0):
        base = SIDE * ((y + jnp.where(core == 0, n, SIDE - n)) % SIDE)
        cols += [base + pair, base + x]
    place = jnp.stack([core, expert] + cols).astype(jnp.int32)
    gate_up = pltpu.with_memory_space_constraint(gate_up, pltpu.HBM)
    down = pltpu.with_memory_space_constraint(down, pltpu.HBM)
    hidden = down.shape[2]
    (weights,) = on_chip(
        hold_kernel,
        "hold",
        (place, gate_up, down),
        [((3, width, hidden), BF16)],
        [pltpu.SemaphoreType.DMA((3,))],
        2,
    )
    swap = lambda piece: [piece, lax.ppermute(piece, "core", SWAP)]
    pieces = swap(line)
    span = line.shape[0]
    forwarded = lambda count: [((3, count * span, hidden), BF16), ((count * span, LANES), F32)]
    h0, gp0 = on_chip(early_kernel, "forward", (place, sel, weights, *pieces, mine[1]), forwarded(3))
    *mine[1:], h0 = lax.optimization_barrier((*mine[1:], h0))
    others = [swap(piece)[1] for piece in mine[1:]]
    h1, gp1 = on_chip(early_kernel, "forward_mine", (place, sel, weights, *mine[2:]), forwarded(2))
    pieces += mine[1:] + others
    moving = lambda steps: ((steps, 3, LANES, hidden), BF16)
    turned = pltpu.VMEM((2, 2 * LANES, len(pieces) * span), BF16)
    h2, gp2, other, own = on_chip(
        functools.partial(late_kernel, (3, 2)),
        "forward_and_first",
        (place, sel, weights, h0, h1, *pieces),
        forwarded(3) + [moving(1)] * 2,
        [turned],
    )

    ring = lambda rows: lax.ppermute(rows, ("y", "core"), RING)
    other, own = ring(other[0]), ring(own[0])
    half = 2 * SIDE * tokens
    rows = ((half, width + LANES), BF16)
    other_next, own_next, part, away = on_chip(
        functools.partial(slot_kernel, tokens, 3),
        "second_and_slots",
        (place, sel, weights, h0, h1, h2, gp0, gp1, gp2, *pieces),
        [moving(1), moving(1), rows, rows],
        [turned, pltpu.VMEM((2, 2 * half, hidden), BF16)],
    )
    other, h2 = lax.optimization_barrier((add(other_next[0], other), h2))
    other = ring(other)
    rest = on_chip(
        functools.partial(rest_kernel, len(pieces), width),
        "weight_terms",
        (place, *pieces, h0, h1, h2),
        [moving(2), moving(2)],
        [turned],
    )
    own, rest = lax.optimization_barrier((own, rest))
    own = ring(add(own_next[0], own))

    away = lax.ppermute(away, ("x", "core"), X_PAIR)
    other, away = lax.optimization_barrier((add(rest[0][0], other), away))
    part = add(part, away)
    half = part.shape[0] // 2
    part = add(part[:half], lax.ppermute(part[half:], "core", SWAP))
    part = part.reshape((SIDE, tokens, part.shape[1]))
    total = part[0].astype(F32)
    for n in range(3):
        total = total + lax.ppermute(part[n + 1], "z", Z_MOVE[n]).astype(F32)
    grad_input = total[:, :width].astype(BF16)
    grad_prob = jnp.sum(jnp.where(hot, total[:, None, width:], 0.0), axis=2)

    other, own = ring(other), ring(add(rest[1][0], own))
    other = lax.ppermute(add(rest[0][1], other), ("x", "core"), X_PAIR)
    own = add(rest[1][1], own)
    even, odd = jnp.where(expert == 0, own, other), jnp.where(expert == 0, other, own)
    grad_weights = jnp.transpose(jnp.stack([even, odd], axis=0), (2, 1, 0, 3))
    return (grad_input, grad_prob, grad_weights)


def solution(mesh):
    grid = Mesh(mesh.devices.reshape(4, 4, 4, 2), ("y", "x", "z", "core"))
    every = P(("y", "x", "z", "core"), None)
    return jax.shard_map(
        shards,
        mesh=grid,
        in_specs=(every, every, every, every, P(None, None, ("z", "core"), None), P(None, ("z", "core"), None)),
        out_specs=(every, every, P(("y", "x"), None, ("z", "core"), None)),
        check_vma=False,
    )
```

```python
import functools

import jax
import jax.numpy as jnp
from jax import lax
from jax.experimental import pallas as pl
from jax.experimental.pallas import tpu as pltpu
from jax.sharding import Mesh, PartitionSpec as P

F32 = jnp.float32
BF16 = jnp.bfloat16
LANES = 128
SIDE = 4
VMEM = 12 << 20
LIGHT = pl.CostEstimate(flops=1 << 20, bytes_accessed=1 << 16, transcendentals=0)

X_ORDER = ((1, 3, 2), (3, 1, 2))
Z_ORDER = (1, 3, 2)
PAIR = (1, 3)


def plane(step, first):
    pairs = []
    for x in range(SIDE):
        for z in range(SIDE):
            for core in range(2):
                if (core == 0) == first:
                    to = (x ^ X_ORDER[core][step], z)
                else:
                    to = (x, z ^ Z_ORDER[step])
                pairs.append(((x * SIDE + z) * 2 + core, (to[0] * SIDE + to[1]) * 2 + core))
    return pairs


SWAP = [(0, 1), (1, 0)]
Z_MOVE = [[(j, j ^ k) for j in range(SIDE)] for k in Z_ORDER]
X_PAIR = [(x * 2 + c, (x ^ PAIR[c]) * 2 + c) for x in range(SIDE) for c in range(2)]
LAST = [
    ((y * SIDE + x) * 2 + c, (((y + 1 - 2 * c) % SIDE) * SIDE + (x ^ PAIR[c])) * 2 + c)
    for y in range(SIDE)
    for x in range(SIDE)
    for c in range(2)
]
RING = [(y * 2 + c, ((y + 1 - 2 * c) % SIDE) * 2 + c) for y in range(SIDE) for c in range(2)]


def hold_kernel(place_ref, gate_up_ref, down_ref, held_ref, sem):
    expert = place_ref[1]
    sources = (gate_up_ref.at[0, expert], gate_up_ref.at[1, expert], down_ref.at[expert])
    copies = [pltpu.make_async_copy(source, held_ref.at[n], sem.at[n]) for n, source in enumerate(sources)]
    for copy in copies:
        copy.start()
    for copy in copies:
        copy.wait()


def forward_rows(row_refs, size, sel_ref, weights_ref, h_ref, gp_ref):
    half = row_refs[0].shape[0]
    _, width, hidden = weights_ref.shape
    tile = 256
    gp_ref[...] = jnp.zeros_like(gp_ref)

    def step(j, carry):
        cols = pl.ds(pl.multiple_of(j * tile, tile), tile)
        for first in range(0, len(row_refs), size):
            pair = row_refs[first : first + size]
            rows = slice(half * first, half * (first + size))
            x = jnp.concatenate([r[:, :width] for r in pair], axis=0)
            dy = jnp.concatenate([r[:, width : 2 * width] for r in pair], axis=0)
            p = jnp.concatenate([r[:, 2 * width :] for r in pair], axis=0).astype(F32)
            p = jnp.sum(p * sel_ref[...], axis=-1, keepdims=True)
            gate = jnp.dot(x, weights_ref[0, :, cols], preferred_element_type=F32)
            up = jnp.dot(x, weights_ref[1, :, cols], preferred_element_type=F32)
            back = jnp.dot(dy, weights_ref[2, :, cols], preferred_element_type=F32)
            sig = 1.0 / (1.0 + jnp.exp(-gate))
            act = gate * sig
            hid = act * up
            hidden_grad = p * back
            h_ref[0, rows, cols] = (hidden_grad * up * (sig * (1.0 + gate * (1.0 - sig)))).astype(BF16)
            h_ref[1, rows, cols] = (hidden_grad * act).astype(BF16)
            h_ref[2, rows, cols] = (p * hid).astype(BF16)
            term = hid * back
            gp_ref[rows] += term[:, :LANES] + term[:, LANES:]
        return carry

    lax.fori_loop(0, hidden // tile, step, 0)


def weight_rows(width, start, cols_ref, row_refs, h_refs, other_ref, own_ref, rows_ref):
    half = row_refs[0].shape[0]

    def step(r, carry):
        for n in range(2):
            for m in range(2):
                at = pl.ds(pl.multiple_of(cols_ref[2 + 2 * (start + r) + m] * LANES + n * width, LANES), LANES)
                for piece, ref in enumerate(row_refs):
                    rows_ref[n, m * LANES : (m + 1) * LANES, half * piece : half * (piece + 1)] = ref[:, at].T
        for kind in range(3):
            total = None
            first = 0
            for h in h_refs:
                span = slice(first, first + h.shape[1])
                first += h.shape[1]
                term = jnp.dot(rows_ref[kind // 2, :, span], h[kind], preferred_element_type=F32)
                total = term if total is None else total + term
            other_ref[r, kind] = total[:LANES].astype(BF16)
            own_ref[r, kind] = total[LANES:].astype(BF16)
        return carry

    lax.fori_loop(0, other_ref.shape[0], step, 0)


def early_kernel(place_ref, sel_ref, weights_ref, *refs):
    *row_refs, h_ref, gp_ref = refs
    forward_rows(row_refs, len(row_refs), sel_ref, weights_ref, h_ref, gp_ref)


def late_kernel(old, place_ref, sel_ref, weights_ref, *refs):
    h_refs, refs = refs[: len(old)], refs[len(old) :]
    row_refs, (h_ref, gp_ref, other_ref, own_ref, turned_ref) = refs[:-5], refs[-5:]
    last = row_refs[sum(old) :]
    forward_rows(last, len(last), sel_ref, weights_ref, h_ref, gp_ref)
    hs = (*h_refs, h_ref)
    weight_rows(weights_ref.shape[1], 0, place_ref, row_refs, hs, other_ref, own_ref, turned_ref)


def rest_kernel(count, width, place_ref, *refs):
    row_refs, h_refs, (other_ref, own_ref, rows_ref) = refs[:count], refs[count:-3], refs[-3:]
    weight_rows(width, 2, place_ref, row_refs, h_refs, other_ref, own_ref, rows_ref)


def on_chip(kernel, name, args, outs, scratch=(), far=0):
    vmem = pl.BlockSpec(memory_space=pltpu.VMEM)
    return pl.pallas_call(
        kernel,
        name=name,
        in_specs=[pl.BlockSpec(memory_space=pltpu.SMEM)]
        + [pl.BlockSpec(memory_space=pl.ANY)] * far
        + [vmem] * (len(args) - 1 - far),
        out_specs=[vmem] * len(outs),
        out_shape=[jax.ShapeDtypeStruct(*out) for out in outs],
        scratch_shapes=list(scratch),
        compiler_params=pltpu.CompilerParams(vmem_limit_bytes=VMEM),
        cost_estimate=LIGHT,
    )(*args)


def slot_rows(core, tokens):
    order = []
    for x in range(2):
        for which in range(2):
            place = 0 if x == 0 else 1 + which
            for z in range(SIDE):
                block, inner = (z, place) if which == core else (place, z)
                if block == 0 or which == 0 and block == 1:
                    chunk, at = 0, which + 2 * block
                else:
                    chunk, at = (2, block - 1) if which else (1, block - 2)
                order.append((chunk, (at * SIDE + inner) * tokens))
    return order


def slot_kernel(tokens, chunks, place_ref, sel_ref, weights_ref, *refs):
    hs, gps, refs = refs[:chunks], refs[chunks : 2 * chunks], refs[2 * chunks :]
    row_refs, (next_other_ref, next_own_ref, own_ref, pair_ref, turned_ref, rows_ref) = refs[:-6], refs[-6:]
    _, width, hidden = weights_ref.shape
    weight_rows(width, 1, place_ref, row_refs, hs, next_other_ref, next_own_ref, turned_ref)
    half = own_ref.shape[0]
    for core in range(2):

        @pl.when(place_ref[0] == core)
        def _():
            for n, (chunk, at) in enumerate(slot_rows(core, tokens)):
                to = slice(n * tokens, (n + 1) * tokens)
                rows_ref[:, to] = hs[chunk][:2, at : at + tokens]
                out, first = (own_ref, 0) if n * tokens < half else (pair_ref, half)
                gp = jnp.sum(gps[chunk][at : at + tokens], axis=-1, keepdims=True) * sel_ref[...]
                out[n * tokens - first : (n + 1) * tokens - first, width:] = gp.astype(BF16)

    contract = (((1,), (1,)), ((), ()))
    tile = 256

    def step(j, carry):
        cols = pl.ds(pl.multiple_of(j * tile, tile), tile)
        total = lax.dot_general(
            rows_ref[0], weights_ref[0, cols], contract, preferred_element_type=F32
        ) + lax.dot_general(rows_ref[1], weights_ref[1, cols], contract, preferred_element_type=F32)
        own_ref[:, cols] = total[:half].astype(BF16)
        pair_ref[:, cols] = total[half:].astype(BF16)
        return carry

    lax.fori_loop(0, width // tile, step, 0)


def add(*terms):
    total = terms[0].astype(F32)
    for term in terms[1:]:
        total = total + term.astype(F32)
    return total.astype(BF16)


def shards(layer_input, out_grad, routes, probs, gate_up, down_t):
    tokens, width = layer_input.shape
    x, y = lax.axis_index("x"), lax.axis_index("y")
    z, core = lax.axis_index("z"), lax.axis_index("core")
    expert = x % 2
    lane = lax.broadcasted_iota(jnp.int32, (1, LANES), 1)
    sel = (lane == (z * 2 + core) * 2 + expert).astype(F32)

    hot = routes.T[:, None, :] == lax.broadcasted_iota(jnp.int32, (1, LANES, 1), 1)
    dense = jnp.sum(jnp.where(hot, probs.T.astype(F32)[:, None, :], 0.0), axis=0).astype(BF16).T
    row = jnp.concatenate([layer_input, out_grad, dense], axis=1)

    axes = ("x", "z", "core")
    down = jnp.transpose(down_t, (1, 0, 2))
    line = [row] + [lax.ppermute(row, axes, plane(n, True)) for n in range(3)]
    line = jnp.concatenate(line, axis=0)
    line, down = lax.optimization_barrier((line, down))
    mine = [line] + [lax.ppermute(line, axes, plane(n, False)) for n in range(3)]

    gate_up = jnp.transpose(gate_up, (1, 2, 0, 3))

    cols = []
    pair = x ^ jnp.where(core == 0, PAIR[0], PAIR[1])
    for n in (3, 2, 1, 0):
        base = SIDE * ((y + jnp.where(core == 0, n, SIDE - n)) % SIDE)
        cols += [base + pair, base + x]
    place = jnp.stack([core, expert] + cols).astype(jnp.int32)
    gate_up = pltpu.with_memory_space_constraint(gate_up, pltpu.HBM)
    down = pltpu.with_memory_space_constraint(down, pltpu.HBM)
    hidden = down.shape[2]
    (weights,) = on_chip(
        hold_kernel,
        "hold",
        (place, gate_up, down),
        [((3, width, hidden), BF16)],
        [pltpu.SemaphoreType.DMA((3,))],
        2,
    )
    swap = lambda piece: [piece, lax.ppermute(piece, "core", SWAP)]
    pieces = swap(line)
    span = line.shape[0]
    forwarded = lambda count: [((3, count * span, hidden), BF16), ((count * span, LANES), F32)]
    h0, gp0 = on_chip(early_kernel, "forward", (place, sel, weights, *pieces, mine[1]), forwarded(3))
    *mine[1:], h0 = lax.optimization_barrier((*mine[1:], h0))
    others = [swap(piece)[1] for piece in mine[1:]]
    h1, gp1 = on_chip(early_kernel, "forward_mine", (place, sel, weights, *mine[2:]), forwarded(2))
    pieces += mine[1:] + others
    moving = lambda steps: ((steps, 3, LANES, hidden), BF16)
    turned = pltpu.VMEM((2, 2 * LANES, len(pieces) * span), BF16)
    h2, gp2, other, own = on_chip(
        functools.partial(late_kernel, (3, 2)),
        "forward_and_first",
        (place, sel, weights, h0, h1, *pieces),
        forwarded(3) + [moving(1)] * 2,
        [turned],
    )

    ring = lambda rows: lax.ppermute(rows, ("y", "core"), RING)
    other, own = ring(other[0]), ring(own[0])
    half = 2 * SIDE * tokens
    rows = ((half, width + LANES), BF16)
    other_next, own_next, part, away = on_chip(
        functools.partial(slot_kernel, tokens, 3),
        "second_and_slots",
        (place, sel, weights, h0, h1, h2, gp0, gp1, gp2, *pieces),
        [moving(1), moving(1), rows, rows],
        [turned, pltpu.VMEM((2, 2 * half, hidden), BF16)],
    )
    other, h2 = lax.optimization_barrier((add(other_next[0], other), h2))
    other = ring(other)
    rest = on_chip(
        functools.partial(rest_kernel, len(pieces), width),
        "weight_terms",
        (place, *pieces, h0, h1, h2),
        [moving(2), moving(2)],
        [turned],
    )
    own, rest = lax.optimization_barrier((own, rest))
    own = ring(add(own_next[0], own))

    away = lax.ppermute(away, ("x", "core"), X_PAIR)
    other, away = lax.optimization_barrier((add(rest[0][0], other), away))
    part = add(part, away)
    half = part.shape[0] // 2
    part = add(part[:half], lax.ppermute(part[half:], "core", SWAP))
    part = part.reshape((SIDE, tokens, part.shape[1]))
    total = part[0].astype(F32)
    for n in range(3):
        total = total + lax.ppermute(part[n + 1], "z", Z_MOVE[n]).astype(F32)
    grad_input = total[:, :width].astype(BF16)
    grad_prob = jnp.sum(jnp.where(hot, total[:, width:].T[None], 0.0), axis=1).T

    home = lax.ppermute(rest[0][1], ("x", "core"), X_PAIR)
    other, own = lax.ppermute(other, ("y", "x", "core"), LAST), ring(add(rest[1][0], own))
    other = add(home, other)
    own = add(rest[1][1], own)
    even, odd = jnp.where(expert == 0, own, other), jnp.where(expert == 0, other, own)
    grad_weights = jnp.transpose(jnp.stack([even, odd], axis=0), (2, 1, 0, 3))
    return (grad_input, grad_prob, grad_weights)


def solution(mesh):
    grid = Mesh(mesh.devices.reshape(4, 4, 4, 2), ("y", "x", "z", "core"))
    every = P(("y", "x", "z", "core"), None)
    return jax.shard_map(
        shards,
        mesh=grid,
        in_specs=(every, every, every, every, P(None, None, ("z", "core"), None), P(None, ("z", "core"), None)),
        out_specs=(every, every, P(("y", "x"), None, ("z", "core"), None)),
        check_vma=False,
    )
```
